32 devices in a mesh: groups: 2 (over x), rows: 16 (over z, y, core).
Axes of the slice: x: 2, y: 2, z: 4, core: 2. Of those that a mesh axis runs over, the one named last changes fastest.
Arguments:
- points: bfloat16 [64, 32768], P(None, ('groups', 'rows')), parts along dimension 1, may hold values from -12 to 12
- landmarks: bfloat16 [64, 2048], P(None, 'groups'), parts along dimension 1, may hold values from -12 to 12
- chol: float32 [2048, 1024], P('groups'), parts along dimension 0, as said below
- ridge: float32 [2], P('groups'), parts along dimension 0, may hold values from 0.5 to 2
- solution: float32 [8, 32768], P(None, ('groups', 'rows')), parts along dimension 1, may hold values from -6 to 6
- residual: float32 [8, 32768], P(None, ('groups', 'rows')), parts along dimension 1, may hold values from -6 to 6
- direction: float32 [8, 32768], P(None, ('groups', 'rows')), parts along dimension 1, may hold values from -6 to 6
- rz_prev: float32 [16], P('groups'), parts along dimension 0, may hold values from 8192 to 32768
Outputs:
- solution_new: float32 [8, 32768], P(None, ('groups', 'rows')), parts along dimension 1
- residual_new: float32 [8, 32768], P(None, ('groups', 'rows')), parts along dimension 1
- direction_new: float32 [8, 32768], P(None, ('groups', 'rows')), parts along dimension 1
- inner_new: float32 [16], P('groups'), parts along dimension 0
The draws below stay inside these ranges and needn't reach their ends.
There are 2 independent parts, one for each index of `groups`. The reference program is written for one: setup_inputs(seed, part) draws one part's arguments, and reference() takes and returns one part's arrays. A program takes and returns all parts, laid end to end along the dimension named above; each array names one. Nothing has to cross between parts.
Inputs may be any that keep to these rules, and one draw needn't show every extreme that they name: chol is lower triangular with a positive diagonal, and chol chol^T = ridge k(landmarks, landmarks) + cross^T cross, with k and cross as in the reference program.
All inputs are finite; a program needn't handle non-finite values.
Results may differ from the reference program's by a relative error of at most 0.0064.
Values may be sent and summed in bfloat16 or wider, within the bound.
No kernel may reach another device: no remote copies, remote signals or barrier semaphores. Data moves between devices by JAX's collectives and lax.ppermute only.
A program may use at most 64 MiB of HBM per device.

```python
import math
import jax
import jax.numpy as jnp
from jax import lax

FEAT = 64
OUTS = 8
LAND = 1024
NPTS = 16384


latent_dims = 8


def shared_sample(key):
    base = jax.random.fold_in(key, 23)
    keys = jax.random.split(base, 6)
    basis = jnp.clip(jax.random.normal(keys[0], (FEAT, latent_dims), jnp.float32), -3.0, 3.0)
    spread = 0.5
    latent_points = jax.random.uniform(keys[1], (latent_dims, NPTS), jnp.float32, -1.5, 1.5)
    latent_marks = jax.random.uniform(keys[2], (latent_dims, LAND), jnp.float32, -1.5, 1.5)
    ridge_value = jnp.exp(jax.random.uniform(keys[5], (1,), jnp.float32, math.log(0.5), math.log(2.0)))
    noise_points = spread * jnp.clip(jax.random.normal(keys[3], (FEAT, NPTS), jnp.float32), -4.0, 4.0)
    noise_marks = spread * jnp.clip(jax.random.normal(keys[4], (FEAT, LAND), jnp.float32), -4.0, 4.0)
    points = jnp.clip(jnp.dot(basis, latent_points, precision=lax.Precision.HIGHEST) + noise_points, -12.0, 12.0)
    landmarks = jnp.clip(jnp.dot(basis, latent_marks, precision=lax.Precision.HIGHEST) + noise_marks, -12.0, 12.0)
    return (points, landmarks, ridge_value)


def square_sums(values):
    return jnp.sum(values * values, axis=0)


def gauss_kernel(left, right):
    inner = jnp.dot(left.T, right, precision=lax.Precision.HIGHEST)
    dist = square_sums(left)[:, None] + square_sums(right)[None, :] - 2.0 * inner
    return jnp.exp(-dist / (2.0 * FEAT))


def draw_points(key, part):
    return shared_sample(key)[0].astype(jnp.bfloat16)


def draw_landmarks(key, part):
    return shared_sample(key)[1].astype(jnp.bfloat16)


def draw_ridge(key, part):
    return shared_sample(key)[2].astype(jnp.float32)


def draw_chol(key, part):
    points, landmarks, ridge_value = shared_sample(key)
    rounded_points = points.astype(jnp.bfloat16).astype(jnp.float32)
    rounded_marks = landmarks.astype(jnp.bfloat16).astype(jnp.float32)
    cross = gauss_kernel(rounded_points, rounded_marks)
    inner = ridge_value[0] * gauss_kernel(rounded_marks, rounded_marks)
    inner = inner + jnp.dot(cross.T, cross, precision=lax.Precision.HIGHEST)
    inner = 0.5 * (inner + inner.T)
    return jnp.linalg.cholesky(inner).astype(jnp.float32)


def block_levels(rng, extent, cuts, smallest, top_value):
    loudness = 1.0
    for position, shards_of in cuts:
        draws = jax.random.uniform(jax.random.fold_in(jax.random.fold_in(rng, 6), position), (shards_of,), jnp.float32, smallest / len(cuts), top_value / len(cuts))
        loudness = loudness * jnp.repeat(jnp.exp(draws), extent[position] // shards_of).reshape((-1,) + (1,) * (len(extent) - 1 - position))
    return loudness


def gaussian(rng, dims, width, bound, shards=(), held_as=jnp.bfloat16):
    gain = block_levels(rng, dims, shards, -0.22, 0.18) if shards else 1.0
    values = jax.random.normal(rng, dims, jnp.float32) * width * gain
    return jnp.minimum(jnp.maximum(values, -bound), bound).astype(held_as)


def setup_inputs(seed: int = 0, part: int = 0) -> dict:
    splits = jax.random.split(jax.random.key(seed), 9)
    part_keys = jax.random.split(jax.random.fold_in(splits[8], part), 9)
    return {
        "points": draw_points(jax.random.fold_in(jax.random.fold_in(splits[8], part), 71), part),
        "landmarks": draw_landmarks(jax.random.fold_in(jax.random.fold_in(splits[8], part), 71), part),
        "chol": draw_chol(jax.random.fold_in(jax.random.fold_in(splits[8], part), 71), part),
        "ridge": draw_ridge(jax.random.fold_in(jax.random.fold_in(splits[8], part), 71), part),
        "solution": gaussian(part_keys[4], (OUTS, NPTS), 1.0, 6.0, ((1, 16),), jnp.float32),
        "residual": gaussian(part_keys[5], (OUTS, NPTS), 1.0, 6.0, ((1, 16),), jnp.float32),
        "direction": gaussian(part_keys[6], (OUTS, NPTS), 1.0, 6.0, ((1, 16),), jnp.float32),
        "rz_prev": jnp.clip(jnp.exp(jax.random.uniform(part_keys[7], (OUTS,), jnp.float32, math.log(8192.0), math.log(32768.0))), 8192.0, 32768.0),
    }


def square_norms(features):
    wide = features.astype(jnp.float32)
    return jnp.sum(wide * wide, axis=0)

def kernel_block(row_points, row_norms, col_points, col_norms):
    scale = 0.5 / row_points.shape[0]
    cross = lax.dot_general(row_points.astype(jnp.float32), col_points.astype(jnp.float32), (((0,), (0,)), ((), ())), preferred_element_type=jnp.float32)
    dist = row_norms[:, None] + col_norms[None, :] - 2.0 * cross
    return jnp.exp(-scale * dist)

def reference(points, landmarks, chol, ridge, solution, residual, direction, rz_prev):
    ridge_value = ridge[0]
    norms = square_norms(points)
    landmark_norms = square_norms(landmarks)
    landmark_kernel = kernel_block(points, norms, landmarks, landmark_norms)
    projection = jnp.dot(residual, landmark_kernel, precision=lax.Precision.HIGHEST)
    coeffs = jax.scipy.linalg.cho_solve((chol, True), projection.T)
    precond = (residual - jnp.dot(coeffs.T, landmark_kernel.T, precision=lax.Precision.HIGHEST)) / ridge_value
    inner_new = jnp.sum(precond * residual, axis=1)
    direction_new = precond + (inner_new / rz_prev)[:, None] * direction
    direction_low = direction_new.astype(jnp.bfloat16)
    total = points.shape[1]
    block_len = math.gcd(total, 512)
    blocks = total // block_len
    feature_count = points.shape[0]
    point_blocks = jnp.moveaxis(points.reshape(feature_count, blocks, block_len), 1, 0)
    norm_blocks = norms.reshape(blocks, block_len)

    def one_block(inputs):
        block_points, block_norms = inputs
        kernel_tile = kernel_block(block_points, block_norms, points, norms).astype(jnp.bfloat16)
        return lax.dot_general(direction_low.astype(jnp.float32), kernel_tile.astype(jnp.float32), (((1,), (1,)), ((), ())), preferred_element_type=jnp.float32)
    stacked = lax.map(one_block, (point_blocks, norm_blocks))
    kernel_part = jnp.moveaxis(stacked, 0, 1).reshape(direction_new.shape[0], total)
    image = kernel_part + ridge_value * direction_new
    curvature = jnp.sum(direction_new * image, axis=1)
    alpha = inner_new / curvature
    solution_new = solution + alpha[:, None] * direction_new
    residual_new = residual - alpha[:, None] * image
    return (solution_new, residual_new, direction_new, inner_new)
```

```python
import functools
import math

import jax
import jax.numpy as jnp
from jax import lax
from jax.experimental import pallas as pl
from jax.experimental.pallas import tpu as pltpu
from jax.sharding import PartitionSpec as P

F32 = jnp.float32
B16 = jnp.bfloat16
LOG2E = 1.4426950408889634
PAD = 10
VMEM = pl.BlockSpec(memory_space=pltpu.VMEM)
SMEM = pl.BlockSpec(memory_space=pltpu.SMEM)
HIGH = lax.Precision.HIGHEST


def dot(a, b, ca, cb, precision=None):
    return lax.dot_general(
        a, b, (((ca,), (cb,)), ((), ())), precision=precision, preferred_element_type=F32
    )


def split3(x):
    hi = x.astype(B16)
    rest = x - hi.astype(F32)
    mid = rest.astype(B16)
    low = (rest - mid.astype(F32)).astype(B16)
    return hi, mid, low


def norm_rows(features):
    wide = features.astype(F32)
    return split3(jnp.sum(wide * wide, axis=0, keepdims=True))


def rows_side(features):
    n = features.shape[1]
    hi, mid, low = norm_rows(features)
    return jnp.concatenate(
        [features, hi, mid, low, jnp.ones((3, n), B16), jnp.zeros((PAD, n), B16)], axis=0
    )


def cols_side(features):
    n = features.shape[1]
    hi, mid, low = norm_rows(features)
    return jnp.concatenate(
        [features * 2, -jnp.ones((3, n), B16), -hi, -mid, -low, jnp.zeros((PAD, n), B16)], axis=0
    )


def gauss(exponent, features):
    return jnp.exp2(exponent * (0.5 * LOG2E / features))


def cross_kernel(pts_ref, marks_ref, res_ref, cross_ref, proj_ref):
    feat = pts_ref.shape[0]
    land = marks_ref.shape[1]
    exponent = dot(rows_side(pts_ref[...]), cols_side(marks_ref[...]), 0, 0)
    cross = gauss(exponent, feat)
    cross_ref[...] = cross
    res = res_ref[...]
    proj_ref[:, :land] = dot(res, cross, 1, 0, HIGH)
    squares = jnp.sum(res * res, axis=1, keepdims=True)
    proj_ref[:, land:] = jnp.broadcast_to(squares, (res.shape[0], proj_ref.shape[1] - land))


def inverse_kernel(chol_ref, inv_ref):
    size = chol_ref.shape[0]
    base = math.gcd(size, 128)
    row = lax.broadcasted_iota(jnp.int32, (base, base), 0)
    col = lax.broadcasted_iota(jnp.int32, (base, base), 1)
    eye = row == col
    count = size // base
    inv_ref[...] = jnp.zeros((size, size), F32)
    blocks, inverses = [], []
    for b in range(count):
        lo = b * base
        block = chol_ref[lo : lo + base, lo : lo + base]
        diag = jnp.where(eye, block, 0.0)
        inv_col = 1.0 / jnp.sum(diag, axis=1, keepdims=True)
        inv_row = 1.0 / jnp.sum(diag, axis=0, keepdims=True)
        pair = (row // 2 == col // 2) & (row > col)
        scaled = inv_col * inv_row
        x = jnp.where(eye, inv_col, 0.0) - jnp.where(pair, block * scaled, 0.0)
        blocks.append(block)
        inverses.append(x)
    step = 2
    while step < base:
        mask = (row // (2 * step) == col // (2 * step)) & (row // step > col // step)
        tmp = [dot(jnp.where(mask, blocks[b], 0.0), inverses[b], 1, 0, HIGH) for b in range(count)]
        inverses = [inverses[b] - dot(inverses[b], tmp[b], 1, 0, HIGH) for b in range(count)]
        step *= 2
    for b in range(count):
        lo = b * base
        inv_ref[lo : lo + base, lo : lo + base] = inverses[b]
    step = base
    while step < size:
        tmp = []
        for lo in range(0, size, 2 * step):
            mid, end = lo + step, lo + 2 * step
            tmp.append(dot(chol_ref[mid:end, lo:mid], inv_ref[lo:mid, lo:mid], 1, 0, HIGH))
        for i, lo in enumerate(range(0, size, 2 * step)):
            mid, end = lo + step, lo + 2 * step
            inv_ref[mid:end, lo:mid] = -dot(inv_ref[mid:end, mid:end], tmp[i], 1, 0, HIGH)
        step *= 2


def direction_kernel(ridge_ref, rz_ref, proj_ref, inv_ref, cross_ref, res_ref, dir_ref, new_ref, low_ref, inner_ref):
    land = cross_ref.shape[1]
    ridge = ridge_ref[0]
    proj = proj_ref[:, :land]
    squares = proj_ref[:, land : land + 1]
    half = dot(proj, inv_ref[...], 1, 1, HIGH)
    coeffs = dot(half, inv_ref[...], 1, 0, HIGH)
    inner = (squares - jnp.sum(proj * coeffs, axis=1, keepdims=True)) / ridge
    precond = (res_ref[...] - dot(coeffs, cross_ref[...], 1, 1, HIGH)) / ridge
    new = precond + (inner / rz_ref[...]) * dir_ref[...]
    new_ref[...] = new
    low_ref[...] = new.astype(B16)
    inner_ref[...] = inner


def image_kernel(points_at, ridge_ref, own_ref, pts_ref, low_ref, new_ref, image_ref, curv_ref, lhs_ref):
    feat, width = own_ref.shape
    blocks = len(points_at)
    group = math.gcd(blocks, 4)
    lhs_ref[...] = cols_side(own_ref[...])
    total = jnp.zeros(image_ref.shape, F32)
    for first in range(0, blocks, group):
        pts = jnp.concatenate(
            [pts_ref[:, points_at[b] * width : (points_at[b] + 1) * width] for b in range(first, first + group)],
            axis=1,
        )
        kernel = gauss(dot(rows_side(pts), lhs_ref[...], 0, 0), feat).astype(B16)
        total = total + dot(low_ref[:, first * width : (first + group) * width], kernel, 1, 0)
    new = new_ref[...]
    image = total + ridge_ref[0] * new
    image_ref[...] = image
    curv = jnp.sum(new * image, axis=1, keepdims=True)
    curv_ref[...] = jnp.broadcast_to(curv, curv_ref.shape)


def exchange(x, mask, count):
    return lax.ppermute(x, "rows", [(i, i ^ mask) for i in range(count)])


def stages(count):
    out, bit = [], 1
    while bit < count:
        if 2 * bit < count:
            out.append([bit, 2 * bit, 3 * bit])
            bit *= 4
        else:
            out.append([bit])
            bit *= 2
    return out


def all_sum(x, count):
    for masks in stages(count):
        parts = [x] + [exchange(x, m, count) for m in masks]
        while len(parts) > 1:
            parts = [parts[i] + parts[i + 1] for i in range(0, len(parts), 2)]
        x = parts[0]
    return x


def gather(x, stage_list, count):
    order = [0]
    for masks in stage_list:
        x = jnp.concatenate([x] + [exchange(x, m, count) for m in masks], axis=1)
        order = order + [m ^ o for m in masks for o in order]
    return x, order


def call(kernel, out, *args, smem=(), scratch=(), name=None, **cost):
    return pl.pallas_call(
        kernel,
        out_shape=out,
        in_specs=[SMEM if i in smem else VMEM for i in range(len(args))],
        out_specs=jax.tree.map(lambda _: VMEM, out),
        scratch_shapes=list(scratch),
        compiler_params=pltpu.CompilerParams(vmem_limit_bytes=56 * 2**20),
        name=name,
    )(*args)


def local(count, points, landmarks, chol, ridge, solution, residual, direction, rz_prev):
    outs, width = residual.shape
    land = landmarks.shape[1]
    shape = jax.ShapeDtypeStruct
    *lower, top = stages(count)
    point_stages = [top] + [[masks[i]] for masks in reversed(lower) for i in range(len(masks) // 2, -1, -1)]
    all_points, point_order = gather(points, point_stages, count)
    cross, partial = call(
        cross_kernel,
        (shape((width, land), F32), shape((outs, land + 128), F32)),
        points, landmarks, residual, name="cross",
    )
    inverse = call(inverse_kernel, shape((land, land), F32), chol, name="inverse")
    proj = all_sum(partial, count)
    new, low, inner = call(
        direction_kernel,
        (shape((outs, width), F32), shape((outs, width), B16), shape((outs, 1), F32)),
        ridge, rz_prev[:, None], proj, inverse, cross, residual, direction, smem=(0,), name="direction",
    )
    all_low, low_order = gather(low, stages(count), count)
    points_at = [point_order.index(m) for m in low_order]
    image, curv = call(
        functools.partial(image_kernel, points_at),
        (shape((outs, width), F32), shape((outs, 128), F32)),
        ridge, points, all_points, all_low, new, smem=(0,),
        scratch=(pltpu.VMEM((points.shape[0] + 6 + PAD, width), B16),), name="image",
    )
    curv = all_sum(curv, count)
    inner_new = inner[:, 0]
    alpha = inner / curv[:, :1]
    return (solution + alpha * new, residual - alpha * image, new, inner_new)


def solution(mesh):
    count = mesh.shape["rows"]
    vec = P(None, ("groups", "rows"))
    in_specs = (vec, P(None, "groups"), P("groups", None), P("groups"), vec, vec, vec, P("groups"))
    out_specs = (vec, vec, vec, P("groups"))
    return jax.shard_map(
        functools.partial(local, count), mesh=mesh, in_specs=in_specs, out_specs=out_specs, check_vma=False
    )
```

```python
import functools
import math

import jax
import jax.numpy as jnp
from jax import lax
from jax.experimental import pallas as pl
from jax.experimental.pallas import tpu as pltpu
from jax.sharding import PartitionSpec as P

F32 = jnp.float32
B16 = jnp.bfloat16
LOG2E = 1.4426950408889634
PAD = 10
VMEM = pl.BlockSpec(memory_space=pltpu.VMEM)
ANY = pl.BlockSpec(memory_space=pl.ANY)
SMEM = pl.BlockSpec(memory_space=pltpu.SMEM)
HIGH = lax.Precision.HIGHEST


def dot(a, b, ca, cb, precision=None):
    return lax.dot_general(
        a, b, (((ca,), (cb,)), ((), ())), precision=precision, preferred_element_type=F32
    )


def split3(x):
    hi = x.astype(B16)
    rest = x - hi.astype(F32)
    mid = rest.astype(B16)
    low = (rest - mid.astype(F32)).astype(B16)
    return hi, mid, low


def norm_rows(features):
    wide = features.astype(F32)
    return split3(jnp.sum(wide * wide, axis=0, keepdims=True))


def rows_side(features):
    n = features.shape[1]
    hi, mid, low = norm_rows(features)
    return jnp.concatenate(
        [features, hi, mid, low, jnp.ones((3, n), B16), jnp.zeros((PAD, n), B16)], axis=0
    )


def cols_side(features):
    n = features.shape[1]
    hi, mid, low = norm_rows(features)
    return jnp.concatenate(
        [features * 2, -jnp.ones((3, n), B16), -hi, -mid, -low, jnp.zeros((PAD, n), B16)], axis=0
    )


def gauss(exponent, features):
    return jnp.exp2(exponent * (0.5 * LOG2E / features))


def stacked(x):
    return jnp.concatenate([piece.astype(F32) for piece in split3(x)], axis=0).astype(B16)


def wide_dot(x, pieces, axis):
    rows = x.shape[0]
    stack = stacked(x)
    total = None
    for i, piece in enumerate(pieces):
        count = len(pieces) - i
        part = dot(stack[: count * rows] if rows % 16 == 0 else stack, piece, 1, axis)
        for k in reversed(range(count)):
            term = part[k * rows : (k + 1) * rows]
            total = term if total is None else total + term
    return total


def fine_dot(a, b):
    n = b.shape[1]
    ah, am, al = split3(a)
    bh, bm, bl = split3(b)
    both = jnp.concatenate([bh, bm], axis=1)
    first = dot(jnp.concatenate([ah, am], axis=1), jnp.concatenate([both, both], axis=0), 1, 0)
    second = dot(jnp.concatenate([ah, al], axis=1), jnp.concatenate([bl, bh], axis=0), 1, 0)
    return (second + first[:, n:]) + first[:, :n]


def cross_kernel(pts_ref, marks_ref, res_ref, *refs):
    cross_refs, proj_ref = refs[:-1], refs[-1]
    feat = pts_ref.shape[0]
    land = marks_ref.shape[1]
    exponent = dot(rows_side(pts_ref[...]), cols_side(marks_ref[...]), 0, 0)
    pieces = split3(gauss(exponent, feat))
    for ref, piece in zip(cross_refs, pieces):
        ref[...] = piece
    res = res_ref[...]
    proj_ref[:, :land] = wide_dot(res, pieces, 0)
    squares = jnp.sum(res * res, axis=1, keepdims=True)
    proj_ref[:, land:] = jnp.broadcast_to(squares, (res.shape[0], proj_ref.shape[1] - land))


def inverse_kernel(chol_ref, *inv_refs):
    half = inv_refs[0].shape[1]
    size = chol_ref.shape[0]
    base = math.gcd(half, 128)
    row = lax.broadcasted_iota(jnp.int32, (base, base), 0)
    col = lax.broadcasted_iota(jnp.int32, (base, base), 1)
    eye = row == col
    count = size // base
    blocks, inverses = [], []
    for b in range(count):
        lo = b * base
        block = chol_ref[lo : lo + base, lo : lo + base]
        diag = jnp.where(eye, block, 0.0)
        inv_col = 1.0 / jnp.sum(diag, axis=1, keepdims=True)
        inv_row = 1.0 / jnp.sum(diag, axis=0, keepdims=True)
        pair = (row // 2 == col // 2) & (row > col)
        x = jnp.where(eye, inv_col, 0.0) - jnp.where(pair, block * (inv_col * inv_row), 0.0)
        blocks.append(block)
        inverses.append(x)
    step = 2
    while step < base:
        mask = (row // (2 * step) == col // (2 * step)) & (row // step > col // step)
        tmp = [fine_dot(jnp.where(mask, blocks[b], 0.0), inverses[b]) for b in range(count)]
        inverses = [inverses[b] - fine_dot(inverses[b], tmp[b]) for b in range(count)]
        step *= 2
    while step < half:
        tmp = []
        for i in range(0, count, 2):
            lo = i * step
            tmp.append(fine_dot(chol_ref[lo + step : lo + 2 * step, lo : lo + step], inverses[i]))
        merged = []
        for i in range(0, count, 2):
            low = -fine_dot(inverses[i + 1], tmp[i // 2])
            top = jnp.concatenate([inverses[i], jnp.zeros((step, step), F32)], axis=1)
            merged.append(jnp.concatenate([top, jnp.concatenate([low, inverses[i + 1]], axis=1)], axis=0))
        inverses = merged
        count //= 2
        step *= 2
    for i in range(count):
        for ref, piece in zip(inv_refs, split3(inverses[i])):
            ref[i * half : (i + 1) * half, :] = piece


def direction_kernel(ridge_ref, rz_ref, *refs):
    proj_refs, refs = refs[:4], refs[4:]
    chol_ref, refs = refs[0], refs[1:]
    inv_refs, cross_refs, refs = refs[:3], refs[3:6], refs[6:]
    res_ref, dir_ref, new_ref, low_ref, inner_ref = refs
    land = cross_refs[0].shape[1]
    half = inv_refs[0].shape[1]
    ridge = ridge_ref[0]
    lane = lax.broadcasted_iota(jnp.int32, inner_ref.shape, 0)
    rz = sum(jnp.where(lane == i, rz_ref[i], 0.0) for i in range(inner_ref.shape[0]))
    sums = (proj_refs[0][...] + proj_refs[1][...]) + (proj_refs[2][...] + proj_refs[3][...])
    proj = sums[:, :land]
    squares = sums[:, land : land + 1]
    below = split3(chol_ref[half:, :half])
    upper = [ref[:half] for ref in inv_refs]
    lower = [ref[half:] for ref in inv_refs]
    y0 = wide_dot(proj[:, :half], upper, 1)
    y1 = wide_dot(proj[:, half:] - wide_dot(y0, below, 1), lower, 1)
    x1 = wide_dot(y1, lower, 0)
    x0 = wide_dot(y0 - wide_dot(x1, below, 0), upper, 0)
    coeffs = jnp.concatenate([x0, x1], axis=1)
    inner = (squares - jnp.sum(proj * coeffs, axis=1, keepdims=True)) / ridge
    precond = (res_ref[...] - wide_dot(coeffs, [ref[...] for ref in cross_refs], 1)) / ridge
    new = precond + (inner / rz) * dir_ref[...]
    new_ref[...] = new
    low_ref[...] = new.astype(B16)
    inner_ref[...] = inner


def products(points_at, first, own_lhs, pts_ref, low_ref, total):
    feat, width = pts_ref.shape[0], own_lhs.shape[1]
    group = math.gcd(len(points_at), 4)
    for i in range(0, len(points_at), group):
        pts = jnp.concatenate(
            [pts_ref[:, at * width : (at + 1) * width] for at in points_at[i : i + group]], axis=1
        )
        kernel = gauss(dot(rows_side(pts), own_lhs[...], 0, 0), feat).astype(B16)
        at = (first + i) * width
        total = total + dot(low_ref[:, at : at + group * width], kernel, 1, 0)
    return total


def near_kernel(points_at, own_ref, pts_ref, low_ref, total_ref, lhs_ref):
    lhs_ref[...] = cols_side(own_ref[...])
    total_ref[...] = products(points_at, 0, lhs_ref, pts_ref, low_ref, jnp.zeros(total_ref.shape, F32))


def image_kernel(points_at, first, ridge_ref, own_ref, pts_ref, low_ref, near_ref, new_ref, image_ref, curv_ref, lhs_ref):
    lhs_ref[...] = cols_side(own_ref[...])
    total = products(points_at, first, lhs_ref, pts_ref, low_ref, near_ref[...])
    new = new_ref[...]
    image = total + ridge_ref[0] * new
    image_ref[...] = image
    curv = jnp.sum(new * image, axis=1, keepdims=True)
    curv_ref[...] = jnp.broadcast_to(curv, curv_ref.shape)


def update_kernel(*refs):
    curv_refs, refs = refs[:4], refs[4:]
    inner_ref, sol_ref, res_ref, new_ref, image_ref, sol_out, res_out, inner_out = refs
    curv = (curv_refs[0][...] + curv_refs[1][...]) + (curv_refs[2][...] + curv_refs[3][...])
    inner = inner_ref[...]
    alpha = inner / curv[:, :1]
    n = inner.shape[0]
    eye = lax.broadcasted_iota(jnp.int32, (n, n), 0) == lax.broadcasted_iota(jnp.int32, (n, n), 1)
    inner_out[...] = jnp.sum(jnp.where(eye, inner, 0.0), axis=0, keepdims=True)
    sol_out[...] = sol_ref[...] + alpha * new_ref[...]
    res_out[...] = res_ref[...] - alpha * image_ref[...]


def exchange(x, mask, count):
    return lax.ppermute(x, "rows", [(i, i ^ mask) for i in range(count)])


def stages(count):
    out, bit = [], 1
    while bit < count:
        if 2 * bit < count:
            out.append([bit, 2 * bit, 3 * bit])
            bit *= 4
        else:
            out.append([bit])
            bit *= 2
    return out


def add_kernel(*refs):
    parts = [ref[...] for ref in refs[:-1]]
    while len(parts) > 1:
        parts = [parts[i] + parts[i + 1] for i in range(0, len(parts), 2)]
    refs[-1][...] = parts[0]


def join_kernel(*refs):
    at = 0
    for ref in refs[:-1]:
        refs[-1][:, at : at + ref.shape[1]] = ref[...]
        at += ref.shape[1]


def add_up(parts, after=()):
    return call(add_kernel, jax.ShapeDtypeStruct(parts[0].shape, F32), *parts, name="add", room=1, after=after)


def join(parts, after=()):
    rows, dtype = parts[0].shape[0], parts[0].dtype
    total = sum(part.shape[1] for part in parts)
    return call(join_kernel, jax.ShapeDtypeStruct((rows, total), dtype), *parts, name="join", room=8, after=after)


def all_sum(x, level_list, count, after=()):
    for masks in level_list:
        x = add_up(x, after) if isinstance(x, list) else x
        x = [x] + [exchange(x, m, count) for m in masks]
    return x + [jnp.zeros_like(x[0])] * (4 - len(x))


def gather(x, order, level_list, count, afters=()):
    for i, masks in enumerate(level_list):
        x = join([x] + [exchange(x, m, count) for m in masks], afters[i] if i < len(afters) else ())
        order = order + [m ^ o for m in masks for o in order]
    return x, order


def call(kernel, out, *args, smem=(), scratch=(), name=None, work=0, room=16, after=()):
    body = (lambda *refs: kernel(*refs[len(after) :])) if after else kernel
    smem = [i + len(after) for i in smem]
    args = tuple(after) + args
    return pl.pallas_call(
        body,
        out_shape=out,
        in_specs=[
            ANY if i < len(after) else SMEM if i in smem else VMEM for i in range(len(args))
        ],
        out_specs=jax.tree.map(lambda _: VMEM, out),
        scratch_shapes=list(scratch),
        compiler_params=pltpu.CompilerParams(vmem_limit_bytes=room * 2**20),
        cost_estimate=pl.CostEstimate(flops=2 * work, bytes_accessed=0, transcendentals=0),
        name=name,
    )(*args)


def local(count, points, landmarks, chol, ridge, solution, residual, direction, rz_prev):
    feat = points.shape[0]
    outs, width = residual.shape
    land = landmarks.shape[1]
    shape = jax.ShapeDtypeStruct
    depth = 256
    levels = stages(count)
    side = pltpu.VMEM((feat + 6 + PAD, width), B16)
    *lower, top = levels
    far_stages = [[m] for masks in reversed(lower) for m in masks[1::-1]]
    *cross, partial = call(
        cross_kernel,
        (shape((width, land), B16),) * 3 + (shape((outs, land + 128), F32),),
        points, landmarks, residual, name="cross", room=24, work=5 * width * land * depth,
    )
    inverse = call(
        inverse_kernel, (shape((land, land // 2), B16),) * 3, chol,
        name="inverse", work=width * land * depth, after=(partial,),
    )
    partial = add_up(all_sum(partial, levels[:1], count), inverse[:1])
    near_points, near_order = gather(points, [0], [top], count, [(partial,)])
    proj = all_sum(partial, levels[1:], count)
    new, low, inner = call(
        direction_kernel,
        (shape((outs, width), F32), shape((outs, width), B16), shape((outs, 1), F32)),
        ridge, rz_prev, *proj, chol, *inverse, *cross, residual, direction,
        smem=(0, 1), name="direction", room=24, work=6 * width * land * depth,
    )
    all_points, point_order = gather(near_points, near_order, far_stages, count, [(new,)])
    near_low, low_order = gather(low, [0], [top], count)
    near = call(
        functools.partial(near_kernel, [near_order.index(m) for m in low_order]),
        shape((outs, width), F32),
        points, near_points, near_low, scratch=(side,), name="near", room=32,
        work=2 * len(low_order) * width * width * depth,
    )
    first = len(low_order)
    all_low, low_order = gather(near_low, low_order, lower[::-1], count, [(near,)])
    image, curv = call(
        functools.partial(image_kernel, [point_order.index(m) for m in low_order[first:]], first),
        (shape((outs, width), F32), shape((outs, 128), F32)),
        ridge, points, all_points, all_low, near, new, smem=(0,),
        scratch=(side,), name="image", room=32, work=2 * (count - first) * width * width * depth,
    )
    sol_new, res_new, inner_row = call(
        update_kernel,
        (shape((outs, width), F32),) * 2 + (shape((1, outs), F32),),
        *all_sum(curv, levels, count), inner, solution, residual, new, image, name="update",
    )
    return (sol_new, res_new, new, inner_row.reshape(outs))


def solution(mesh):
    count = mesh.shape["rows"]
    vec = P(None, ("groups", "rows"))
    in_specs = (vec, P(None, "groups"), P("groups", None), P("groups"), vec, vec, vec, P("groups"))
    out_specs = (vec, vec, vec, P("groups"))
    return jax.shard_map(
        functools.partial(local, count), mesh=mesh, in_specs=in_specs, out_specs=out_specs, check_vma=False
    )
```

```python
import functools
import math

import jax
import jax.numpy as jnp
from jax import lax
from jax.experimental import pallas as pl
from jax.experimental.pallas import tpu as pltpu
from jax.sharding import PartitionSpec as P

F32 = jnp.float32
B16 = jnp.bfloat16
LOG2E = 1.4426950408889634
PAD = 10
VMEM = pl.BlockSpec(memory_space=pltpu.VMEM)
ANY = pl.BlockSpec(memory_space=pl.ANY)
SMEM = pl.BlockSpec(memory_space=pltpu.SMEM)
HIGH = lax.Precision.HIGHEST


def dot(a, b, ca, cb, precision=None):
    return lax.dot_general(
        a, b, (((ca,), (cb,)), ((), ())), precision=precision, preferred_element_type=F32
    )


def split3(x):
    hi = x.astype(B16)
    rest = x - hi.astype(F32)
    mid = rest.astype(B16)
    low = (rest - mid.astype(F32)).astype(B16)
    return hi, mid, low


def norm_rows(features):
    wide = features.astype(F32)
    return split3(jnp.sum(wide * wide, axis=0, keepdims=True))


def rows_side(features):
    n = features.shape[1]
    hi, mid, low = norm_rows(features)
    return jnp.concatenate(
        [features, hi, mid, low, jnp.ones((3, n), B16), jnp.zeros((PAD, n), B16)], axis=0
    )


def cols_side(features):
    n = features.shape[1]
    hi, mid, low = norm_rows(features)
    return jnp.concatenate(
        [features * 2, -jnp.ones((3, n), B16), -hi, -mid, -low, jnp.zeros((PAD, n), B16)], axis=0
    )


def gauss(exponent, features):
    return jnp.exp2(exponent * (0.5 * LOG2E / features))


def on_diagonal(rows, lanes):
    shape = (rows, lanes)
    return lax.broadcasted_iota(jnp.int32, shape, 0) == lax.broadcasted_iota(jnp.int32, shape, 1)


def to_lanes(column):
    return jnp.sum(jnp.where(on_diagonal(column.shape[0], 128), column, 0.0), axis=0, keepdims=True)


def to_rows(row, count):
    return jnp.sum(jnp.where(on_diagonal(count, row.shape[1]), row, 0.0), axis=1, keepdims=True)


def stacked(x):
    return jnp.concatenate([piece.astype(F32) for piece in split3(x)], axis=0).astype(B16)


def wide_dot(x, pieces, axis):
    rows = x.shape[0]
    stack = stacked(x)
    total = None
    for i, piece in enumerate(pieces):
        count = 3 - i
        part = dot(stack[: count * rows] if rows % 16 == 0 else stack, piece, 1, axis)
        for k in reversed(range(count)):
            term = part[k * rows : (k + 1) * rows]
            total = term if total is None else total + term
    return total


def fine_dot(a, b):
    n = b.shape[1]
    ah, am, al = split3(a)
    bh, bm, bl = split3(b)
    both = jnp.concatenate([bh, bm], axis=1)
    first = dot(jnp.concatenate([ah, am], axis=1), jnp.concatenate([both, both], axis=0), 1, 0)
    second = dot(jnp.concatenate([ah, al], axis=1), jnp.concatenate([bl, bh], axis=0), 1, 0)
    return (second + first[:, n:]) + first[:, :n]


def cross_kernel(pts_ref, marks_ref, res_ref, *refs):
    cross_refs, refs = refs[:2], refs[2:]
    proj_ref = refs[0]
    feat = pts_ref.shape[0]
    land = marks_ref.shape[1]
    exponent = dot(rows_side(pts_ref[...]), cols_side(marks_ref[...]), 0, 0)
    pieces = split3(gauss(exponent, feat))[: len(cross_refs)]
    for ref, piece in zip(cross_refs, pieces):
        ref[...] = piece
    res = res_ref[...]
    proj_ref[:, :land] = wide_dot(res, pieces, 0)
    squares = jnp.sum(res * res, axis=1, keepdims=True)
    proj_ref[:, land:] = jnp.broadcast_to(squares, (res.shape[0], proj_ref.shape[1] - land))


def inverse_kernel(chol_ref, inv_ref):
    size, base = inv_ref.shape
    row = lax.broadcasted_iota(jnp.int32, (base, base), 0)
    col = lax.broadcasted_iota(jnp.int32, (base, base), 1)
    eye = row == col
    count = size // base
    blocks, inverses = [], []
    for b in range(count):
        lo = b * base
        block = chol_ref[lo : lo + base, lo : lo + base]
        diag = jnp.where(eye, block, 0.0)
        inv_col = 1.0 / jnp.sum(diag, axis=1, keepdims=True)
        inv_row = 1.0 / jnp.sum(diag, axis=0, keepdims=True)
        pair = (row // 2 == col // 2) & (row > col)
        x = jnp.where(eye, inv_col, 0.0) - jnp.where(pair, block * (inv_col * inv_row), 0.0)
        blocks.append(block)
        inverses.append(x)
    step = 2
    while step < base:
        mask = (row // (2 * step) == col // (2 * step)) & (row // step > col // step)
        tmp = [fine_dot(jnp.where(mask, blocks[b], 0.0), inverses[b]) for b in range(count)]
        inverses = [inverses[b] - fine_dot(inverses[b], tmp[b]) for b in range(count)]
        step *= 2
    for b in range(count):
        inv_ref[b * base : (b + 1) * base, :] = inverses[b]


def merge_kernel(chol_ref, part_ref, *inv_refs):
    size, step = chol_ref.shape[0], part_ref.shape[1]
    inverses = [part_ref[lo : lo + step, :] for lo in range(0, size, step)]
    while len(inverses) > 1:
        merged = []
        for i in range(0, len(inverses), 2):
            lo, zero = i * step, jnp.zeros((step, step), F32)
            block, cut = chol_ref[lo + step : lo + 2 * step, lo : lo + step], step // 2
            low = fine_dot(block, inverses[i]) if step < 256 else jnp.concatenate(
                [fine_dot(block, inverses[i][:, :cut]), fine_dot(block[:, cut:], inverses[i][cut:, cut:])], axis=1
            )
            other = inverses[i + 1]
            low = -(fine_dot(other, low) if step < 256 else jnp.concatenate(
                [fine_dot(other[:cut, :cut], low[:cut]), fine_dot(other[cut:], low)], axis=0
            ))
            if len(inverses) == 2:
                for ref, c, nw, sw, se in zip(inv_refs, split3(zero), split3(inverses[0]), split3(low), split3(inverses[1])):
                    ref[:step, :step] = nw
                    ref[:step, step:] = c
                    ref[step:, :step] = sw
                    ref[step:, step:] = se
                return
            top = jnp.concatenate([inverses[i], zero], axis=1)
            merged.append(jnp.concatenate([top, jnp.concatenate([low, inverses[i + 1]], axis=1)], axis=0))
        inverses = merged
        step *= 2


def direction_kernel(ridge_ref, rz_ref, *refs):
    proj_refs, refs = refs[:4], refs[4:]
    inv_refs, cross_refs, refs = refs[:3], refs[3:5], refs[5:]
    res_ref, dir_ref, new_ref, near_ref, low_ref, inner_ref = refs
    land = cross_refs[0].shape[1]
    half = land // 2
    ridge = ridge_ref[0]
    lane = lax.broadcasted_iota(jnp.int32, inner_ref.shape, 0)
    rz = sum(jnp.where(lane == i, rz_ref[i], 0.0) for i in range(inner_ref.shape[0]))
    sums = (proj_refs[0][...] + proj_refs[1][...]) + (proj_refs[2][...] + proj_refs[3][...])
    proj = sums[:, :land]
    squares = sums[:, land : land + 1]
    north = [ref[:half, :half] for ref in inv_refs]
    south = [ref[half:] for ref in inv_refs]
    y0 = wide_dot(proj[:, :half], north, 1)
    y1 = wide_dot(proj, south, 1)
    x0 = wide_dot(jnp.concatenate([y0, y1], axis=1), [ref[:, :half] for ref in inv_refs], 0)
    x1 = wide_dot(y1, [ref[half:, half:] for ref in inv_refs], 0)
    coeffs = jnp.concatenate([x0, x1], axis=1)
    inner = (squares - jnp.sum(proj * coeffs, axis=1, keepdims=True)) / ridge
    precond = (res_ref[...] - wide_dot(coeffs, [ref[...] for ref in cross_refs], 1)) / ridge
    new = precond + (inner / rz) * dir_ref[...]
    new_ref[...] = new
    near_ref[...] = new
    low_ref[...] = new.astype(B16)
    inner_ref[...] = inner


def tile(pts, lhs):
    return gauss(dot(rows_side(pts), lhs, 0, 0), pts.shape[0]).astype(B16)


def tiles_kernel(first, own_ref, pts_ref, tiles_ref):
    width = own_ref.shape[1]
    lhs = cols_side(own_ref[...])
    group = math.gcd(tiles_ref.shape[0] // width, 2)
    for at in range(0, tiles_ref.shape[0], group * width):
        pts = pts_ref[:, first * width + at : first * width + at + group * width]
        tiles_ref[at : at + group * width, :] = tile(pts, lhs)


def near_kernel(low_ref, tiles_ref, total_ref):
    total_ref[...] = dot(low_ref[...], tiles_ref[: low_ref.shape[1], :], 1, 0)


def image_kernel(
    low_at, near, ridge_ref, own_ref, pts_ref, low_ref, near_ref, early_ref, late_ref, new_ref, image_ref, curv_ref, lhs_ref
):
    width = own_ref.shape[1]
    lhs_ref[...] = cols_side(own_ref[...])

    def low(blocks):
        return jnp.concatenate(
            [low_ref[:, low_at[b] * width : (low_at[b] + 1) * width].astype(F32) for b in blocks], axis=1
        ).astype(B16)

    early = early_ref.shape[0] // width
    held = early + late_ref.shape[0] // width
    blocks = len(low_at)
    total = near_ref[...]
    left = blocks - held
    group = max(g for g in range(1, 3) if left % g == 0)
    for b in range(held, blocks, group):
        pts = pts_ref[:, b * width : (b + group) * width]
        total = total + dot(low(range(b, b + group)), tile(pts, lhs_ref[...]), 1, 0)
    total = total + dot(low(range(near, early)), early_ref[near * width :, :], 1, 0)
    total = total + dot(low(range(early, held)), late_ref[...], 1, 0)
    new = new_ref[...]
    image = total + ridge_ref[0] * new
    image_ref[...] = image
    curv = jnp.sum(new * image, axis=1, keepdims=True)
    curv_ref[...] = jnp.broadcast_to(to_lanes(curv)[None], curv_ref.shape)


def update_kernel(*refs):
    curv_ref, refs = refs[0], refs[1:]
    inner_ref, sol_ref, res_ref, new_ref, image_ref, sol_out, res_out, inner_out = refs
    curv = to_rows(jnp.sum(curv_ref[...], axis=0), inner_ref.shape[0])
    inner = inner_ref[...]
    alpha = inner / curv
    inner_out[...] = to_lanes(inner)[:, : inner.shape[0]]
    sol_out[...] = sol_ref[...] + alpha * new_ref[...]
    res_out[...] = res_ref[...] - alpha * image_ref[...]


def exchange(x, mask, count):
    return lax.ppermute(x, "rows", [(i, i ^ mask) for i in range(count)])


def stages(count):
    out, bit = [], 1
    while bit < count:
        if 2 * bit < count:
            out.append([bit, 2 * bit, 3 * bit])
            bit *= 4
        else:
            out.append([bit])
            bit *= 2
    return out


def add_kernel(*refs):
    parts = [ref[...] for ref in refs[:-1]]
    while len(parts) > 1:
        parts = [parts[i] + parts[i + 1] for i in range(0, len(parts), 2)]
    refs[-1][...] = parts[0]


def join_kernel(*refs):
    at = 0
    for ref in refs[:-1]:
        refs[-1][:, at : at + ref.shape[1]] = ref[...]
        at += ref.shape[1]


def add_up(parts, after=()):
    return call(add_kernel, jax.ShapeDtypeStruct(parts[0].shape, F32), *parts, name="add", room=1, after=after)


def join(parts, after=()):
    rows, dtype = parts[0].shape[0], parts[0].dtype
    total = sum(part.shape[1] for part in parts)
    return call(join_kernel, jax.ShapeDtypeStruct((rows, total), dtype), *parts, name="join", room=8, after=after)


def all_sum(x, level_list, count, after=()):
    for masks in level_list:
        x = add_up(x, after) if isinstance(x, list) else x
        x = [x] + [exchange(x, m, count) for m in masks]
    return x + [jnp.zeros_like(x[0])] * (4 - len(x))


def gather(x, order, level_list, count, afters=()):
    for i, masks in enumerate(level_list):
        x = join([x] + [exchange(x, m, count) for m in masks], afters[i] if i < len(afters) else ())
        order = order + [m ^ o for m in masks for o in order]
    return x, order


def call(kernel, out, *args, smem=(), scratch=(), name=None, work=0, room=16, after=()):
    body = (lambda *refs: kernel(*refs[len(after) :])) if after else kernel
    smem = [i + len(after) for i in smem]
    args = tuple(after) + args
    return pl.pallas_call(
        body,
        out_shape=out,
        in_specs=[
            ANY if i < len(after) else SMEM if i in smem else VMEM for i in range(len(args))
        ],
        out_specs=jax.tree.map(lambda _: VMEM, out),
        scratch_shapes=list(scratch),
        compiler_params=pltpu.CompilerParams(vmem_limit_bytes=room * 2**20),
        cost_estimate=pl.CostEstimate(flops=2 * work, bytes_accessed=0, transcendentals=0),
        name=name,
    )(*args)


def local(count, points, landmarks, chol, ridge, solution, residual, direction, rz_prev):
    feat = points.shape[0]
    outs, width = residual.shape
    land = landmarks.shape[1]
    shape = jax.ShapeDtypeStruct
    depth = 256
    levels = stages(count)
    side = pltpu.VMEM((feat + 6 + PAD, width), B16)
    *lower, top = levels
    far_stages = [[m] for masks in reversed(lower) for m in masks[1::-1]]
    *cross, partial = call(
        cross_kernel,
        (shape((width, land), B16),) * 2 + (shape((outs, land + 128), F32),),
        points, landmarks, residual, name="cross", room=24, work=5 * width * land * depth,
    )
    *quick, last = levels[0][:2]
    if quick:
        partial = add_up([partial, exchange(partial, quick[0], count)])
    base = math.gcd(land, 128)
    inverse = call(
        inverse_kernel, shape((land, base), F32), chol, name="inverse", work=width * land * depth, after=(partial,)
    )
    partial = add_up([partial, exchange(partial, last, count)], (inverse,))
    near_points, near_order = gather(points, [0], [top], count, [(partial,)])
    merged = call(
        merge_kernel, (shape((land, land), B16),) * 3, chol, inverse,
        name="merge", work=2 * width * land * depth, room=24, after=(partial,),
    )
    proj = all_sum(partial, levels[1:], count)
    new, new_kept, low, inner = call(
        direction_kernel,
        (shape((outs, width), F32),) * 2 + (shape((outs, width), B16), shape((outs, 1), F32)),
        ridge, rz_prev, *proj, *merged, *cross, residual, direction,
        smem=(0, 1), name="direction", room=24, work=6 * width * land * depth,
    )
    early_points, early_order = gather(near_points, near_order, far_stages[:1], count, [(inner,)])
    early = len(early_order)
    early_tiles = call(
        functools.partial(tiles_kernel, 0), shape((early * width, width), B16), points, early_points,
        name="tiles", room=14, work=early * width * width * depth, after=(inner,),
    )
    near_low, low_order = gather(low, [0], [top], count, [(early_tiles,)])
    near = len(low_order)
    near_sum = call(
        near_kernel, shape((outs, width), F32), near_low, early_tiles, name="near", room=2,
        work=near * width * width * depth // 2,
    )
    all_points, point_order = gather(early_points, early_order, far_stages[1:], count)
    late = 3
    late_tiles = call(
        functools.partial(tiles_kernel, early), shape((late * width, width), B16), points, all_points,
        name="tiles", room=14, work=late * width * width * depth, after=(near_sum,),
    )
    all_low, low_order = gather(near_low, low_order, lower[::-1], count, [(late_tiles,)])
    image, curv = call(
        functools.partial(image_kernel, [low_order.index(m) for m in point_order], near),
        (shape((outs, width), F32), shape((count, 1, 128), F32)),
        ridge, points, all_points, all_low, near_sum, early_tiles, late_tiles, new_kept, smem=(0,),
        scratch=(side,), name="image", room=14, work=2 * (count - early - late) * width * width * depth,
    )
    sol_new, res_new, inner_row = call(
        update_kernel,
        (shape((outs, width), F32),) * 2 + (shape((1, outs), F32),),
        lax.all_to_all(curv, "rows", 0, 0, tiled=True), inner, solution, residual, new_kept, image, name="update",
    )
    return (sol_new, res_new, new, inner_row.reshape(outs))


def solution(mesh):
    count = mesh.shape["rows"]
    vec = P(None, ("groups", "rows"))
    in_specs = (vec, P(None, "groups"), P("groups", None), P("groups"), vec, vec, vec, P("groups"))
    out_specs = (vec, vec, vec, P("groups"))
    return jax.shard_map(
        functools.partial(local, count), mesh=mesh, in_specs=in_specs, out_specs=out_specs, check_vma=False
    )
```

```python
import functools
import math

import jax
import jax.numpy as jnp
from jax import lax
from jax.experimental import pallas as pl
from jax.experimental.pallas import tpu as pltpu
from jax.sharding import PartitionSpec as P

F32 = jnp.float32
B16 = jnp.bfloat16
LOG2E = 1.4426950408889634
PAD = 10
VMEM = pl.BlockSpec(memory_space=pltpu.VMEM)
ANY = pl.BlockSpec(memory_space=pl.ANY)
SMEM = pl.BlockSpec(memory_space=pltpu.SMEM)
HIGH = lax.Precision.HIGHEST


def dot(a, b, ca, cb, precision=None):
    return lax.dot_general(
        a, b, (((ca,), (cb,)), ((), ())), precision=precision, preferred_element_type=F32
    )


def split3(x):
    hi = x.astype(B16)
    rest = x - hi.astype(F32)
    mid = rest.astype(B16)
    low = (rest - mid.astype(F32)).astype(B16)
    return hi, mid, low


def norm_rows(features):
    wide = features.astype(F32)
    return split3(jnp.sum(wide * wide, axis=0, keepdims=True))


def rows_side(features):
    n = features.shape[1]
    hi, mid, low = norm_rows(features)
    return jnp.concatenate(
        [features, hi, mid, low, jnp.ones((3, n), B16), jnp.zeros((PAD, n), B16)], axis=0
    )


def cols_side(features):
    n = features.shape[1]
    hi, mid, low = norm_rows(features)
    return jnp.concatenate(
        [features * 2, -jnp.ones((3, n), B16), -hi, -mid, -low, jnp.zeros((PAD, n), B16)], axis=0
    )


def gauss(exponent, features):
    return jnp.exp2(exponent * (0.5 * LOG2E / features))


def on_diagonal(rows, lanes):
    shape = (rows, lanes)
    return lax.broadcasted_iota(jnp.int32, shape, 0) == lax.broadcasted_iota(jnp.int32, shape, 1)


def to_lanes(column):
    return jnp.sum(jnp.where(on_diagonal(column.shape[0], 128), column, 0.0), axis=0, keepdims=True)


def to_rows(row, count):
    return jnp.sum(jnp.where(on_diagonal(count, row.shape[1]), row, 0.0), axis=1, keepdims=True)


def stacked(x):
    return jnp.concatenate([piece.astype(F32) for piece in split3(x)], axis=0).astype(B16)


def wide_dot(x, pieces, axis):
    rows = x.shape[0]
    stack = stacked(x)
    total = None
    for i, piece in enumerate(pieces):
        count = 3 - i
        part = dot(stack[: count * rows] if rows % 16 == 0 else stack, piece, 1, axis)
        for k in reversed(range(count)):
            term = part[k * rows : (k + 1) * rows]
            total = term if total is None else total + term
    return total


def fine_dot(a, b):
    n = b.shape[1]
    ah, am, al = split3(a)
    bh, bm, bl = split3(b)
    both = jnp.concatenate([bh, bm], axis=1)
    first = dot(jnp.concatenate([ah, am], axis=1), jnp.concatenate([both, both], axis=0), 1, 0)
    second = dot(jnp.concatenate([ah, al], axis=1), jnp.concatenate([bl, bh], axis=0), 1, 0)
    return (second + first[:, n:]) + first[:, :n]


def cross_kernel(pts_ref, marks_ref, res_ref, *refs):
    cross_refs, refs = refs[:2], refs[2:]
    proj_ref = refs[0]
    feat = pts_ref.shape[0]
    land = marks_ref.shape[1]
    exponent = dot(rows_side(pts_ref[...]), cols_side(marks_ref[...]), 0, 0)
    pieces = split3(gauss(exponent, feat))[: len(cross_refs)]
    for ref, piece in zip(cross_refs, pieces):
        ref[...] = piece
    res = res_ref[...]
    proj_ref[:, :land] = wide_dot(res, pieces, 0)
    squares = jnp.sum(res * res, axis=1, keepdims=True)
    proj_ref[:, land:] = jnp.broadcast_to(squares, (res.shape[0], proj_ref.shape[1] - land))


def inverse_kernel(chol_ref, inv_ref):
    size, base = inv_ref.shape
    row = lax.broadcasted_iota(jnp.int32, (base, base), 0)
    col = lax.broadcasted_iota(jnp.int32, (base, base), 1)
    eye = row == col
    count = size // base
    blocks, inverses = [], []
    for b in range(count):
        lo = b * base
        block = chol_ref[lo : lo + base, lo : lo + base]
        diag = jnp.where(eye, block, 0.0)
        inv_col = 1.0 / jnp.sum(diag, axis=1, keepdims=True)
        inv_row = 1.0 / jnp.sum(diag, axis=0, keepdims=True)
        pair = (row // 2 == col // 2) & (row > col)
        x = jnp.where(eye, inv_col, 0.0) - jnp.where(pair, block * (inv_col * inv_row), 0.0)
        blocks.append(block)
        inverses.append(x)
    step = 2
    while step < base:
        mask = (row // (2 * step) == col // (2 * step)) & (row // step > col // step)
        tmp = [fine_dot(jnp.where(mask, blocks[b], 0.0), inverses[b]) for b in range(count)]
        inverses = [inverses[b] - fine_dot(inverses[b], tmp[b]) for b in range(count)]
        step *= 2
    for b in range(count):
        inv_ref[b * base : (b + 1) * base, :] = inverses[b]


def merge_kernel(chol_ref, part_ref, *refs):
    inv_refs, below_refs = refs[:3], refs[3:]
    size, step = chol_ref.shape[0], part_ref.shape[1]
    half = inv_refs[0].shape[1]
    inverses = [part_ref[lo : lo + step, :] for lo in range(0, size, step)]
    while step < half:
        merged = []
        for i in range(0, len(inverses), 2):
            lo, zero = i * step, jnp.zeros((step, step), F32)
            block, cut = chol_ref[lo + step : lo + 2 * step, lo : lo + step], step // 2
            other = inverses[i + 1]
            if step < 256:
                low = -fine_dot(other, fine_dot(block, inverses[i]))
            else:
                low = jnp.concatenate(
                    [fine_dot(block, inverses[i][:, :cut]), fine_dot(block[:, cut:], inverses[i][cut:, cut:])], axis=1
                )
                low = -jnp.concatenate([fine_dot(other[:cut, :cut], low[:cut]), fine_dot(other[cut:], low)], axis=0)
            top = jnp.concatenate([inverses[i], zero], axis=1)
            merged.append(jnp.concatenate([top, jnp.concatenate([low, other], axis=1)], axis=0))
        inverses = merged
        step *= 2
    for i, inverse in enumerate(inverses):
        for ref, piece in zip(inv_refs, split3(inverse)):
            ref[i * half : (i + 1) * half, :] = piece
    for ref, piece in zip(below_refs, split3(chol_ref[half:, :half])):
        ref[...] = piece


def add_pairs(parts):
    while len(parts) > 1:
        parts = [parts[i] + parts[i + 1] for i in range(0, len(parts), 2)]
    return parts[0]


def direction_kernel(parts, ridge_ref, rz_ref, *refs):
    proj_refs, refs = refs[:parts], refs[parts:]
    inv_refs, below_refs, cross_refs, refs = refs[:3], refs[3:6], refs[6:8], refs[8:]
    res_ref, dir_ref, new_ref, near_ref, low_ref, inner_ref = refs
    land = cross_refs[0].shape[1]
    half = land // 2
    ridge = ridge_ref[0]
    lane = lax.broadcasted_iota(jnp.int32, inner_ref.shape, 0)
    rz = sum(jnp.where(lane == i, rz_ref[i], 0.0) for i in range(inner_ref.shape[0]))
    sums = add_pairs([ref[...] for ref in proj_refs])
    proj = sums[:, :land]
    squares = sums[:, land : land + 1]
    below = [ref[...] for ref in below_refs]
    upper = [ref[:half] for ref in inv_refs]
    lower = [ref[half:] for ref in inv_refs]
    y0 = wide_dot(proj[:, :half], upper, 1)
    y1 = wide_dot(proj[:, half:] - wide_dot(y0, below, 1), lower, 1)
    x1 = wide_dot(y1, lower, 0)
    x0 = wide_dot(y0 - wide_dot(x1, below, 0), upper, 0)
    coeffs = jnp.concatenate([x0, x1], axis=1)
    inner = (squares - jnp.sum(proj * coeffs, axis=1, keepdims=True)) / ridge
    precond = (res_ref[...] - wide_dot(coeffs, [ref[...] for ref in cross_refs], 1)) / ridge
    new = precond + (inner / rz) * dir_ref[...]
    new_ref[...] = new
    near_ref[...] = new
    low_ref[...] = new.astype(B16)
    inner_ref[...] = inner


def tile(pts, lhs):
    return gauss(dot(rows_side(pts), lhs, 0, 0), pts.shape[0]).astype(B16)


def tiles_kernel(first, own_ref, pts_ref, tiles_ref):
    width = own_ref.shape[1]
    lhs = cols_side(own_ref[...])
    group = math.gcd(tiles_ref.shape[0] // width, 2)
    for at in range(0, tiles_ref.shape[0], group * width):
        pts = pts_ref[:, first * width + at : first * width + at + group * width]
        tiles_ref[at : at + group * width, :] = tile(pts, lhs)


def near_kernel(first, own_ref, pts_ref, low_ref, held_ref, total_ref, tiles_ref):
    total_ref[...] = dot(low_ref[...], held_ref[: low_ref.shape[1], :], 1, 0)
    tiles_kernel(first, own_ref, pts_ref, tiles_ref)


def image_kernel(low_at, near, tile_count, ridge_ref, own_ref, pts_ref, low_ref, near_ref, *refs):
    tile_refs, (new_ref, image_ref, curv_ref, lhs_ref) = refs[:tile_count], refs[tile_count:]
    width = own_ref.shape[1]
    lhs_ref[...] = cols_side(own_ref[...])

    def low(blocks):
        return jnp.concatenate(
            [low_ref[:, low_at[b] * width : (low_at[b] + 1) * width].astype(F32) for b in blocks], axis=1
        ).astype(B16)

    at, total = near, near_ref[...]
    for ref in tile_refs:
        end = at + ref.shape[0] // width
        total = total + dot(low(range(at, end)), ref[...], 1, 0)
        at = end
    blocks = len(low_at)
    group = max(g for g in range(1, 3) if (blocks - at) % g == 0)
    for b in range(at, blocks, group):
        pts = pts_ref[:, b * width : (b + group) * width]
        total = total + dot(low(range(b, b + group)), tile(pts, lhs_ref[...]), 1, 0)
    new = new_ref[...]
    image = total + ridge_ref[0] * new
    image_ref[...] = image
    curv = jnp.sum(new * image, axis=1, keepdims=True)
    curv_ref[...] = jnp.broadcast_to(to_lanes(curv)[None], curv_ref.shape)


def update_kernel(*refs):
    curv_ref, refs = refs[0], refs[1:]
    inner_ref, sol_ref, res_ref, new_ref, image_ref, sol_out, res_out, inner_out = refs
    curv = to_rows(jnp.sum(curv_ref[...], axis=0), inner_ref.shape[0])
    inner = inner_ref[...]
    alpha = inner / curv
    inner_out[...] = to_lanes(inner)[:, : inner.shape[0]]
    sol_out[...] = sol_ref[...] + alpha * new_ref[...]
    res_out[...] = res_ref[...] - alpha * image_ref[...]


def exchange(x, mask, count):
    return lax.ppermute(x, "rows", [(i, i ^ mask) for i in range(count)])


def stages(count):
    out, bit = [], 1
    while bit < count:
        if 2 * bit < count:
            out.append([bit, 2 * bit, 3 * bit])
            bit *= 4
        else:
            out.append([bit])
            bit *= 2
    return out


def add_kernel(*refs):
    refs[-1][...] = add_pairs([ref[...] for ref in refs[:-1]])


def join_kernel(*refs):
    at = 0
    for ref in refs[:-1]:
        refs[-1][:, at : at + ref.shape[1]] = ref[...]
        at += ref.shape[1]


def add_up(parts, after=()):
    return call(add_kernel, jax.ShapeDtypeStruct(parts[0].shape, F32), *parts, name="add", room=1, after=after)


def join(parts, after=()):
    rows, dtype = parts[0].shape[0], parts[0].dtype
    total = sum(part.shape[1] for part in parts)
    return call(join_kernel, jax.ShapeDtypeStruct((rows, total), dtype), *parts, name="join", room=8, after=after)


def all_sum(x, level_list, count, after=()):
    for masks in level_list:
        x = add_up(x, after) if isinstance(x, list) else x
        x = [x] + [exchange(x, m, count) for m in masks]
    return x + [jnp.zeros_like(x[0])] * (4 - len(x))


def gather(x, order, level_list, count, afters=()):
    for i, masks in enumerate(level_list):
        x = join([x] + [exchange(x, m, count) for m in masks], afters[i] if i < len(afters) else ())
        order = order + [m ^ o for m in masks for o in order]
    return x, order


def call(kernel, out, *args, smem=(), scratch=(), name=None, work=0, room=16, after=()):
    body = (lambda *refs: kernel(*refs[len(after) :])) if after else kernel
    smem = [i + len(after) for i in smem]
    args = tuple(after) + args
    return pl.pallas_call(
        body,
        out_shape=out,
        in_specs=[
            ANY if i < len(after) else SMEM if i in smem else VMEM for i in range(len(args))
        ],
        out_specs=jax.tree.map(lambda _: VMEM, out),
        scratch_shapes=list(scratch),
        compiler_params=pltpu.CompilerParams(vmem_limit_bytes=room * 2**20),
        cost_estimate=pl.CostEstimate(flops=2 * work, bytes_accessed=0, transcendentals=0),
        name=name,
    )(*args)


def local(count, points, landmarks, chol, ridge, solution, residual, direction, rz_prev):
    feat = points.shape[0]
    outs, width = residual.shape
    land = landmarks.shape[1]
    shape = jax.ShapeDtypeStruct
    depth = 256
    levels = stages(count)
    side = pltpu.VMEM((feat + 6 + PAD, width), B16)
    *lower, top = levels
    far_stages = [[m] for masks in reversed(lower) for m in masks[1::-1]]
    *cross, partial = call(
        cross_kernel,
        (shape((width, land), B16),) * 2 + (shape((outs, land + 128), F32),),
        points, landmarks, residual, name="cross", room=24, work=5 * width * land * depth,
    )
    *quick, last = levels[0][:2]
    if quick:
        partial = add_up([partial, exchange(partial, quick[0], count)])
    base = math.gcd(land, 128)
    inverse = call(
        inverse_kernel, shape((land, base), F32), chol, name="inverse", work=width * land * depth, after=(partial,)
    )
    partial = add_up([partial, exchange(partial, last, count)], (inverse,))
    near_points, near_order = gather(points, [0], [top], count, [(partial,)])
    merged = call(
        merge_kernel, (shape((land, land // 2), B16),) * 3 + (shape((land // 2, land // 2), B16),) * 3, chol, inverse,
        name="merge", work=2 * width * land * depth, room=24, after=(partial,),
    )
    bits = [m for masks in levels[1:] for m in masks[:2]]
    for i, bit in enumerate(bits):
        proj = [partial, exchange(partial, bit, count)]
        if i < len(bits) - 1:
            partial = add_up(proj, (merged[0],))

    def tiles(first, blocks, pts, *after):
        return call(
            functools.partial(tiles_kernel, first), shape((blocks * width, width), B16), points, pts,
            name="tiles", room=14, work=blocks // 2 * width * width * depth, after=after,
        )

    near = len(near_order)
    held = [tiles(0, near, near_points, partial, merged[0])]
    new, new_kept, low, inner = call(
        functools.partial(direction_kernel, len(proj)),
        (shape((outs, width), F32),) * 2 + (shape((outs, width), B16), shape((outs, 1), F32)),
        ridge, rz_prev, *proj, *merged, *cross, residual, direction,
        smem=(0, 1), name="direction", room=24, after=held[:1], work=6 * width * land * depth,
    )
    early_points, early_order = gather(near_points, near_order, far_stages[:1], count, [(inner,)])
    all_points, point_order = gather(early_points, early_order, far_stages[1:], count)
    held.append(tiles(near, len(early_order) - near, early_points, inner))
    first_low, low_order = gather(low, [0], [[m] for m in top[:1]], count, [held[-1:]])
    held.append(tiles(len(early_order), near, all_points, first_low))
    near_low, low_order = gather(first_low, low_order, [[m] for m in top[1:2]], count, [held[-1:]])
    late = near - 1
    near_sum, late_tiles = call(
        functools.partial(near_kernel, len(early_order) + near),
        (shape((outs, width), F32), shape((late * width, width), B16)),
        points, all_points, near_low, held[0], name="near", room=14, work=(late + 1) * width * width * depth,
    )
    held.append(late_tiles)
    all_low, low_order = gather(near_low, low_order, lower[::-1], count, [held[-1:]])
    image, curv = call(
        functools.partial(image_kernel, [low_order.index(m) for m in point_order], near, len(held) - 1),
        (shape((outs, width), F32), shape((count, 1, 128), F32)),
        ridge, points, all_points, all_low, near_sum, *held[1:], new_kept, smem=(0,),
        scratch=(side,), name="image", room=14, work=(count - near) * width * width * depth,
    )
    sol_new, res_new, inner_row = call(
        update_kernel,
        (shape((outs, width), F32),) * 2 + (shape((1, outs), F32),),
        lax.all_to_all(curv, "rows", 0, 0, tiled=True), inner, solution, residual, new_kept, image, name="update",
    )
    return (sol_new, res_new, new, inner_row.reshape(outs))


def solution(mesh):
    count = mesh.shape["rows"]
    vec = P(None, ("groups", "rows"))
    in_specs = (vec, P(None, "groups"), P("groups", None), P("groups"), vec, vec, vec, P("groups"))
    out_specs = (vec, vec, vec, P("groups"))
    return jax.shard_map(
        functools.partial(local, count), mesh=mesh, in_specs=in_specs, out_specs=out_specs, check_vma=False
    )
```

```python
import functools
import math

import jax
import jax.numpy as jnp
from jax import lax
from jax.experimental import pallas as pl
from jax.experimental.pallas import tpu as pltpu
from jax.sharding import PartitionSpec as P

F32 = jnp.float32
B16 = jnp.bfloat16
LOG2E = 1.4426950408889634
PAD = 10
VMEM = pl.BlockSpec(memory_space=pltpu.VMEM)
ANY = pl.BlockSpec(memory_space=pl.ANY)
SMEM = pl.BlockSpec(memory_space=pltpu.SMEM)
HIGH = lax.Precision.HIGHEST


def dot(a, b, ca, cb, precision=None):
    return lax.dot_general(
        a, b, (((ca,), (cb,)), ((), ())), precision=precision, preferred_element_type=F32
    )


def split3(x):
    hi = x.astype(B16)
    rest = x - hi.astype(F32)
    mid = rest.astype(B16)
    low = (rest - mid.astype(F32)).astype(B16)
    return hi, mid, low


def norm_rows(features):
    wide = features.astype(F32)
    return split3(jnp.sum(wide * wide, axis=0, keepdims=True))


def rows_side(features):
    n = features.shape[1]
    hi, mid, low = norm_rows(features)
    return jnp.concatenate(
        [features, hi, mid, low, jnp.ones((3, n), B16), jnp.zeros((PAD, n), B16)], axis=0
    )


def cols_side(features):
    n = features.shape[1]
    hi, mid, low = norm_rows(features)
    return jnp.concatenate(
        [features * 2, -jnp.ones((3, n), B16), -hi, -mid, -low, jnp.zeros((PAD, n), B16)], axis=0
    )


def gauss(exponent, features):
    return jnp.exp2(exponent * (0.5 * LOG2E / features))


def on_diagonal(rows, lanes):
    shape = (rows, lanes)
    return lax.broadcasted_iota(jnp.int32, shape, 0) == lax.broadcasted_iota(jnp.int32, shape, 1)


def to_lanes(column):
    return jnp.sum(jnp.where(on_diagonal(column.shape[0], 128), column, 0.0), axis=0, keepdims=True)


def to_rows(row, count):
    return jnp.sum(jnp.where(on_diagonal(count, row.shape[1]), row, 0.0), axis=1, keepdims=True)


def stacked(x):
    return jnp.concatenate([piece.astype(F32) for piece in split3(x)], axis=0).astype(B16)


def wide_dot(x, pieces, axis):
    rows = x.shape[0]
    stack = stacked(x)
    total = None
    for i, piece in enumerate(pieces):
        count = 3 - i
        part = dot(stack[: count * rows] if rows % 16 == 0 else stack, piece, 1, axis)
        for k in reversed(range(count)):
            term = part[k * rows : (k + 1) * rows]
            total = term if total is None else total + term
    return total


def fine_dot(a, b):
    n = b.shape[1]
    ah, am, al = split3(a)
    bh, bm, bl = split3(b)
    both = jnp.concatenate([bh, bm], axis=1)
    first = dot(jnp.concatenate([ah, am], axis=1), jnp.concatenate([both, both], axis=0), 1, 0)
    second = dot(jnp.concatenate([ah, al], axis=1), jnp.concatenate([bl, bh], axis=0), 1, 0)
    return (second + first[:, n:]) + first[:, :n]


def cross_kernel(pts_ref, marks_ref, res_ref, *refs):
    cross_refs, refs = refs[:2], refs[2:]
    proj_ref = refs[0]
    feat = pts_ref.shape[0]
    land = marks_ref.shape[1]
    exponent = dot(rows_side(pts_ref[...]), cols_side(marks_ref[...]), 0, 0)
    pieces = split3(gauss(exponent, feat))[: len(cross_refs)]
    for ref, piece in zip(cross_refs, pieces):
        ref[...] = piece
    res = res_ref[...]
    proj_ref[:, :land] = wide_dot(res, pieces, 0)
    squares = jnp.sum(res * res, axis=1, keepdims=True)
    proj_ref[:, land:] = jnp.broadcast_to(squares, (res.shape[0], proj_ref.shape[1] - land))


def inverse_kernel(chol_ref, inv_ref):
    size, base = inv_ref.shape
    row = lax.broadcasted_iota(jnp.int32, (base, base), 0)
    col = lax.broadcasted_iota(jnp.int32, (base, base), 1)
    eye = row == col
    count = size // base
    blocks, inverses = [], []
    for b in range(count):
        lo = b * base
        block = chol_ref[lo : lo + base, lo : lo + base]
        diag = jnp.where(eye, block, 0.0)
        inv_col = 1.0 / jnp.sum(diag, axis=1, keepdims=True)
        inv_row = 1.0 / jnp.sum(diag, axis=0, keepdims=True)
        pair = (row // 2 == col // 2) & (row > col)
        x = jnp.where(eye, inv_col, 0.0) - jnp.where(pair, block * (inv_col * inv_row), 0.0)
        blocks.append(block)
        inverses.append(x)
    step = 2
    while step < base:
        mask = (row // (2 * step) == col // (2 * step)) & (row // step > col // step)
        tmp = [fine_dot(jnp.where(mask, blocks[b], 0.0), inverses[b]) for b in range(count)]
        inverses = [inverses[b] - fine_dot(inverses[b], tmp[b]) for b in range(count)]
        step *= 2
    for b in range(count):
        inv_ref[b * base : (b + 1) * base, :] = inverses[b]


def merge_kernel(chol_ref, part_ref, *refs):
    inv_refs, below_refs = refs[:3], refs[3:]
    size, step = chol_ref.shape[0], part_ref.shape[1]
    half = inv_refs[0].shape[1]
    inverses = [part_ref[lo : lo + step, :] for lo in range(0, size, step)]
    while step < half:
        merged = []
        for i in range(0, len(inverses), 2):
            lo, zero = i * step, jnp.zeros((step, step), F32)
            block, cut = chol_ref[lo + step : lo + 2 * step, lo : lo + step], step // 2
            other = inverses[i + 1]
            if step < 256:
                low = -fine_dot(other, fine_dot(block, inverses[i]))
            else:
                low = jnp.concatenate(
                    [fine_dot(block, inverses[i][:, :cut]), fine_dot(block[:, cut:], inverses[i][cut:, cut:])], axis=1
                )
                low = -jnp.concatenate([fine_dot(other[:cut, :cut], low[:cut]), fine_dot(other[cut:], low)], axis=0)
            top = jnp.concatenate([inverses[i], zero], axis=1)
            merged.append(jnp.concatenate([top, jnp.concatenate([low, other], axis=1)], axis=0))
        inverses = merged
        step *= 2
    for i, inverse in enumerate(inverses):
        for ref, piece in zip(inv_refs, split3(inverse)):
            ref[i * half : (i + 1) * half, :] = piece
    for ref, piece in zip(below_refs, split3(chol_ref[half:, :half])):
        ref[...] = piece


def add_pairs(parts):
    while len(parts) > 1:
        parts = [parts[i] + parts[i + 1] for i in range(0, len(parts), 2)]
    return parts[0]


def direction_kernel(parts, ridge_ref, rz_ref, *refs):
    proj_refs, refs = refs[:parts], refs[parts:]
    inv_refs, below_refs, cross_refs, refs = refs[:3], refs[3:6], refs[6:8], refs[8:]
    res_ref, dir_ref, new_ref, near_ref, low_ref, inner_ref = refs
    land = cross_refs[0].shape[1]
    half = land // 2
    ridge = ridge_ref[...].reshape(1, 1)
    outs = inner_ref.shape[0]
    rz = to_rows(rz_ref[...].reshape(1, outs), outs)
    sums = add_pairs([ref[...] for ref in proj_refs])
    proj = sums[:, :land]
    squares = sums[:, land : land + 1]
    below = [ref[...] for ref in below_refs]
    upper = [ref[:half] for ref in inv_refs]
    lower = [ref[half:] for ref in inv_refs]
    y0 = wide_dot(proj[:, :half], upper, 1)
    y1 = wide_dot(proj[:, half:] - wide_dot(y0, below, 1), lower, 1)
    x1 = wide_dot(y1, lower, 0)
    x0 = wide_dot(y0 - wide_dot(x1, below, 0), upper, 0)
    coeffs = jnp.concatenate([x0, x1], axis=1)
    inner = (squares - jnp.sum(proj * coeffs, axis=1, keepdims=True)) / ridge
    precond = (res_ref[...] - wide_dot(coeffs, [ref[...] for ref in cross_refs], 1)) / ridge
    new = precond + (inner / rz) * dir_ref[...]
    new_ref[...] = new
    near_ref[...] = new
    low_ref[...] = new.astype(B16)
    inner_ref[...] = inner


def tile(pts, lhs):
    return gauss(dot(rows_side(pts), lhs, 0, 0), pts.shape[0]).astype(B16)


def tiles_kernel(first, own_ref, pts_ref, tiles_ref):
    width = own_ref.shape[1]
    lhs = cols_side(own_ref[...])
    group = math.gcd(tiles_ref.shape[0] // width, 2)
    for at in range(0, tiles_ref.shape[0], group * width):
        pts = pts_ref[:, first * width + at : first * width + at + group * width]
        tiles_ref[at : at + group * width, :] = tile(pts, lhs)


def near_kernel(first, own_ref, pts_ref, low_ref, held_ref, total_ref, tiles_ref):
    total_ref[...] = dot(low_ref[...], held_ref[: low_ref.shape[1], :], 1, 0)
    tiles_kernel(first, own_ref, pts_ref, tiles_ref)


def image_kernel(low_at, near, tile_count, ridge_ref, own_ref, pts_ref, low_ref, near_ref, *refs):
    tile_refs, (new_ref, image_ref, curv_ref, lhs_ref) = refs[:tile_count], refs[tile_count:]
    width = own_ref.shape[1]
    lhs_ref[...] = cols_side(own_ref[...])

    def low(blocks):
        return jnp.concatenate(
            [low_ref[:, low_at[b] * width : (low_at[b] + 1) * width].astype(F32) for b in blocks], axis=1
        ).astype(B16)

    at, total = near, near_ref[...]
    for ref in tile_refs:
        end = at + ref.shape[0] // width
        total = total + dot(low(range(at, end)), ref[...], 1, 0)
        at = end
    blocks = len(low_at)
    group = max(g for g in range(1, 3) if (blocks - at) % g == 0)
    for b in range(at, blocks, group):
        pts = pts_ref[:, b * width : (b + group) * width]
        total = total + dot(low(range(b, b + group)), tile(pts, lhs_ref[...]), 1, 0)
    new = new_ref[...]
    image = total + ridge_ref[...].reshape(1, 1) * new
    image_ref[...] = image
    curv = jnp.sum(new * image, axis=1, keepdims=True)
    curv_ref[...] = jnp.broadcast_to(to_lanes(curv)[None], curv_ref.shape)


def update_kernel(*refs):
    curv_ref, refs = refs[0], refs[1:]
    inner_ref, sol_ref, res_ref, new_ref, image_ref, sol_out, res_out, inner_out = refs
    curv = to_rows(jnp.sum(curv_ref[...], axis=0), inner_ref.shape[0])
    inner = inner_ref[...]
    alpha = inner / curv
    inner_out[...] = to_lanes(inner)[:, : inner.shape[0]]
    sol_out[...] = sol_ref[...] + alpha * new_ref[...]
    res_out[...] = res_ref[...] - alpha * image_ref[...]


def exchange(x, mask, count):
    return lax.ppermute(x, "rows", [(i, i ^ mask) for i in range(count)])


def stages(count):
    out, bit = [], 1
    while bit < count:
        if 2 * bit < count:
            out.append([bit, 2 * bit, 3 * bit])
            bit *= 4
        else:
            out.append([bit])
            bit *= 2
    return out


def add_kernel(*refs):
    refs[-1][...] = add_pairs([ref[...] for ref in refs[:-1]])


def join_kernel(*refs):
    at = 0
    for ref in refs[:-1]:
        refs[-1][:, at : at + ref.shape[1]] = ref[...]
        at += ref.shape[1]


def add_up(parts, after=()):
    return call(add_kernel, jax.ShapeDtypeStruct(parts[0].shape, F32), *parts, name="add", room=1, after=after)


def join(parts, after=()):
    rows, dtype = parts[0].shape[0], parts[0].dtype
    total = sum(part.shape[1] for part in parts)
    return call(join_kernel, jax.ShapeDtypeStruct((rows, total), dtype), *parts, name="join", room=8, after=after)


def all_sum(x, level_list, count, after=()):
    for masks in level_list:
        x = add_up(x, after) if isinstance(x, list) else x
        x = [x] + [exchange(x, m, count) for m in masks]
    return x + [jnp.zeros_like(x[0])] * (4 - len(x))


def gather(x, order, level_list, count, afters=()):
    for i, masks in enumerate(level_list):
        x = join([x] + [exchange(x, m, count) for m in masks], afters[i] if i < len(afters) else ())
        order = order + [m ^ o for m in masks for o in order]
    return x, order


def call(kernel, out, *args, smem=(), scratch=(), name=None, work=0, room=16, after=()):
    body = (lambda *refs: kernel(*refs[len(after) :])) if after else kernel
    smem = [i + len(after) for i in smem]
    args = tuple(after) + args
    return pl.pallas_call(
        body,
        out_shape=out,
        in_specs=[
            ANY if i < len(after) else SMEM if i in smem else VMEM for i in range(len(args))
        ],
        out_specs=jax.tree.map(lambda _: VMEM, out),
        scratch_shapes=list(scratch),
        compiler_params=pltpu.CompilerParams(vmem_limit_bytes=room * 2**20),
        cost_estimate=pl.CostEstimate(flops=2 * work, bytes_accessed=0, transcendentals=0),
        name=name,
    )(*args)


def local(count, points, landmarks, chol, ridge, solution, residual, direction, rz_prev):
    feat = points.shape[0]
    outs, width = residual.shape
    land = landmarks.shape[1]
    shape = jax.ShapeDtypeStruct
    depth = 256
    levels = stages(count)
    side = pltpu.VMEM((feat + 6 + PAD, width), B16)
    *lower, top = levels
    far_stages = [[m] for masks in reversed(lower) for m in masks[1::-1]]
    *cross, partial = call(
        cross_kernel,
        (shape((width, land), B16),) * 2 + (shape((outs, land + 128), F32),),
        points, landmarks, residual, name="cross", room=24, work=5 * width * land * depth,
    )
    *quick, last = levels[0][:2]
    if quick:
        partial = add_up([partial, exchange(partial, quick[0], count)])
    base = math.gcd(land, 128)
    inverse = call(
        inverse_kernel, shape((land, base), F32), chol, name="inverse", work=width * land * depth, after=(partial,)
    )
    partial = add_up([partial, exchange(partial, last, count)], (inverse,))
    near_points, near_order = gather(points, [0], [top], count, [(partial,)])
    merged = call(
        merge_kernel, (shape((land, land // 2), B16),) * 3 + (shape((land // 2, land // 2), B16),) * 3, chol, inverse,
        name="merge", work=2 * width * land * depth, room=24, after=(partial,),
    )
    bits = [m for masks in levels[1:] for m in masks[:2]]
    for i, bit in enumerate(bits):
        proj = [partial, exchange(partial, bit, count)]
        if i < len(bits) - 1:
            partial = add_up(proj, (merged[0],))

    def tiles(first, blocks, pts, *after):
        return call(
            functools.partial(tiles_kernel, first), shape((blocks * width, width), B16), points, pts,
            name="tiles", room=14, work=blocks // 2 * width * width * depth, after=after,
        )

    near = len(near_order)
    held = [tiles(0, near, near_points, partial, merged[0])]
    new, new_kept, low, inner = call(
        functools.partial(direction_kernel, len(proj)),
        (shape((outs, width), F32),) * 2 + (shape((outs, width), B16), shape((outs, 1), F32)),
        ridge, rz_prev, *proj, *merged, *cross, residual, direction,
        name="direction", room=24, after=held[:1], work=6 * width * land * depth,
    )
    early_points, early_order = gather(near_points, near_order, far_stages[:1], count, [(inner,)])
    all_points, point_order = gather(early_points, early_order, far_stages[1:], count)
    held.append(tiles(near, len(early_order) - near, early_points, inner))
    first_low, low_order = gather(low, [0], [[m] for m in top[:1]], count, [held[-1:]])
    held.append(tiles(len(early_order), near, all_points, first_low))
    near_low, low_order = gather(first_low, low_order, [[m] for m in top[1:2]], count, [held[-1:]])
    late = near - 1
    near_sum, late_tiles = call(
        functools.partial(near_kernel, len(early_order) + near),
        (shape((outs, width), F32), shape((late * width, width), B16)),
        points, all_points, near_low, held[0], name="near", room=14, work=(late + 1) * width * width * depth,
    )
    held.append(late_tiles)
    all_low, low_order = gather(near_low, low_order, lower[::-1], count, [held[-1:]])
    image, curv = call(
        functools.partial(image_kernel, [low_order.index(m) for m in point_order], near, len(held) - 1),
        (shape((outs, width), F32), shape((count, 1, 128), F32)),
        ridge, points, all_points, all_low, near_sum, *held[1:], new_kept,
        scratch=(side,), name="image", room=14, work=(count - near) * width * width * depth,
    )
    sol_new, res_new, inner_row = call(
        update_kernel,
        (shape((outs, width), F32),) * 2 + (shape((1, outs), F32),),
        lax.all_to_all(curv, "rows", 0, 0, tiled=True), inner, solution, residual, new_kept, image, name="update",
    )
    return (sol_new, res_new, new, inner_row.reshape(outs))


def solution(mesh):
    count = mesh.shape["rows"]
    vec = P(None, ("groups", "rows"))
    in_specs = (vec, P(None, "groups"), P("groups", None), P("groups"), vec, vec, vec, P("groups"))
    out_specs = (vec, vec, vec, P("groups"))
    return jax.shard_map(
        functools.partial(local, count), mesh=mesh, in_specs=in_specs, out_specs=out_specs, check_vma=False
    )
```
